256 devices in a mesh: expert: 64 (over x, y_lo, z), dp: 4 (over y_hi, core).
Axes of the slice: x: 4, y: 4 (y_hi: 2, y_lo: 2; y = y_hi * 2 + y_lo), z: 8, core: 2. Of those that a mesh axis runs over, the one named last changes fastest.
Arguments:
- tokens: bfloat16 [256, 512, 1024], P(('expert', 'dp')), may hold values from -24 to 24
- slot_param: bfloat16 [1024, 64], replicated, may hold values from -2 to 2
- up_weight: bfloat16 [64, 1024, 4096], P('expert', None, 'dp'), may hold values from -0.1875 to 0.1875
- down_weight: bfloat16 [64, 4096, 1024], P('expert', 'dp'), may hold values from -0.09375 to 0.09375
- grad_output: bfloat16 [256, 512, 1024], P(('expert', 'dp')), may hold values from -6 to 6
Outputs:
- grad_tokens: bfloat16 [256, 512, 1024], P(('expert', 'dp'))
- grad_slot_param: float32 [1024, 64], replicated
- grad_up: bfloat16 [64, 1024, 4096], P('expert', None, 'dp')
- grad_down: bfloat16 [64, 4096, 1024], P('expert', 'dp')
The draws below stay inside these ranges and needn't reach their ends.
All inputs are finite; a program needn't handle non-finite values.
Results may differ from the reference program's by a relative error of at most 0.013.
Values may be sent and summed in bfloat16 or wider, within the bound.
No kernel may reach another device: no remote copies, remote signals or barrier semaphores. Data moves between devices by JAX's collectives and lax.ppermute only.
A program may use at most 64 MiB of HBM per device.

```python
import math
import jax
import jax.numpy as jnp
from jax import lax

D = 1024
HID = 4096
TOK = 512
EXPERTS = 64
IMAGES = 256


def base_columns(key):
    values = jax.random.normal(jax.random.fold_in(key, 11), (D, EXPERTS), jnp.float32)
    return jnp.clip(values, -3.0, 3.0) * (3.0 / math.sqrt(D))


def draw_slot_param(key, part):
    columns = base_columns(key)
    return columns.astype(jnp.bfloat16)


def draw_tokens(key, part):
    key = jax.random.fold_in(key, 3)
    keys = jax.random.split(key, 2)
    values = jnp.clip(jax.random.normal(keys[1], (IMAGES, TOK, D), jnp.float32), -6.0, 6.0)
    return values.astype(jnp.bfloat16)


def levels(rng, shape, cuts, least, largest):
    factor_of, own = 1.0, jax.random.fold_in(rng, 6)
    for dim, shards_of in cuts:
        draws = jnp.exp(jax.random.uniform(jax.random.fold_in(own, dim), (shards_of,), jnp.float32, least / len(cuts), largest / len(cuts)))
        factor_of = factor_of * jnp.repeat(draws, shape[dim] // shards_of).reshape([-1 if axis == dim else 1 for axis in range(len(shape))])
    return factor_of


def centred(key, extent, width, reach, pieces=(), kind=jnp.bfloat16):
    result = width * jax.random.normal(key, extent, jnp.float32)
    if pieces:
        result = result * levels(key, extent, pieces, -0.22, 0.18)
    return jnp.clip(result, -reach, reach).astype(kind)


def setup_inputs(seed: int = 0) -> dict:
    arg_keys = jax.random.split(jax.random.key(seed), 6)
    tokens = draw_tokens(jax.random.fold_in(arg_keys[5], 71), 0)
    slot_param = draw_slot_param(jax.random.fold_in(arg_keys[5], 71), 0)
    up_weight = centred(arg_keys[2], (EXPERTS, D, HID), D ** -0.5, 0.1875, ((0, 64), (2, 4)))
    down_weight = centred(arg_keys[3], (EXPERTS, HID, D), HID ** -0.5, 0.09375, ((0, 64), (1, 4)))
    grad_output = centred(arg_keys[4], (IMAGES, TOK, D), 1.0, 6.0, ((0, 256),))
    return {"tokens": tokens, "slot_param": slot_param, "up_weight": up_weight, "down_weight": down_weight, "grad_output": grad_output}


gelu_coeff = 0.7978845608
cubic_coeff = 0.044715


def gelu_tanh(values):
    inner = gelu_coeff * (values + cubic_coeff * values * values * values)
    return 0.5 * values * (1.0 + jnp.tanh(inner))


def gelu_slope(values):
    inner = gelu_coeff * (values + cubic_coeff * values * values * values)
    tangent = jnp.tanh(inner)
    return 0.5 * (1.0 + tangent) + 0.5 * values * (1.0 - tangent * tangent) * gelu_coeff * (1.0 + 3.0 * cubic_coeff * values * values)


def weights_of(image_tokens, slot_param):
    logits = jnp.dot(image_tokens, slot_param, preferred_element_type=jnp.float32)
    dispatch = jax.nn.softmax(logits, axis=0)
    combine = jax.nn.softmax(logits, axis=1)
    return dispatch, combine


def expert_pass(operands):
    rows, grads, first, second = operands
    preact = jnp.dot(rows, first, preferred_element_type=jnp.float32)
    active = gelu_tanh(preact).astype(jnp.bfloat16)
    outputs = jnp.dot(active, second, preferred_element_type=jnp.float32).astype(jnp.bfloat16)
    grad_active = jnp.dot(grads, second.T, preferred_element_type=jnp.float32)
    grad_pre = (grad_active * gelu_slope(preact)).astype(jnp.bfloat16)
    grad_second = jnp.dot(active.T, grads, preferred_element_type=jnp.float32).astype(jnp.bfloat16)
    grad_first = jnp.dot(rows.T, grad_pre, preferred_element_type=jnp.float32).astype(jnp.bfloat16)
    grad_rows = jnp.dot(grad_pre, first.T, preferred_element_type=jnp.float32).astype(jnp.bfloat16)
    return outputs, grad_rows, grad_first, grad_second


def reference(tokens, slot_param, up_weight, down_weight, grad_output):
    def front_image(operands):
        image_tokens, image_grads = operands
        dispatch, combine = weights_of(image_tokens, slot_param)
        dispatch_b = dispatch.astype(jnp.bfloat16)
        combine_b = combine.astype(jnp.bfloat16)
        slot_input = jnp.dot(dispatch_b.T, image_tokens, preferred_element_type=jnp.float32).astype(jnp.bfloat16)
        slot_grad = jnp.dot(combine_b.T, image_grads, preferred_element_type=jnp.float32).astype(jnp.bfloat16)
        return slot_input, slot_grad

    slot_input, slot_grad = lax.map(front_image, (tokens, grad_output))
    outputs, grad_rows, grad_up, grad_down = lax.map(
        expert_pass, (jnp.swapaxes(slot_input, 0, 1), jnp.swapaxes(slot_grad, 0, 1), up_weight, down_weight))
    outputs = jnp.swapaxes(outputs, 0, 1)
    grad_rows = jnp.swapaxes(grad_rows, 0, 1)

    def back_image(carry, operands):
        image_tokens, image_grads, slot_output, slot_in_grad = operands
        dispatch, combine = weights_of(image_tokens, slot_param)
        dispatch_b = dispatch.astype(jnp.bfloat16)
        grad_combine = jnp.dot(image_grads, slot_output.T, preferred_element_type=jnp.float32)
        combine_part = combine * (grad_combine - jnp.sum(combine * grad_combine, axis=1, keepdims=True))
        grad_dispatch = jnp.dot(image_tokens, slot_in_grad.T, preferred_element_type=jnp.float32)
        dispatch_part = dispatch * (grad_dispatch - jnp.sum(dispatch * grad_dispatch, axis=0, keepdims=True))
        grad_logits = (combine_part + dispatch_part).astype(jnp.bfloat16)
        grad_image = jnp.dot(dispatch_b, slot_in_grad, preferred_element_type=jnp.float32)
        grad_image = grad_image + jnp.dot(grad_logits, slot_param.T, preferred_element_type=jnp.float32)
        carry = carry + jnp.dot(image_tokens.T, grad_logits, preferred_element_type=jnp.float32)
        return carry, grad_image.astype(jnp.bfloat16)

    initial = jnp.zeros(slot_param.shape, jnp.float32)
    param_grad, grad_tokens = lax.scan(back_image, initial, (tokens, grad_output, outputs, grad_rows))
    return grad_tokens, param_grad, grad_up, grad_down
```

```python
import jax
import jax.numpy as jnp
from jax import lax
from jax.sharding import Mesh, PartitionSpec as P

gelu_coeff = 0.7978845608
cubic_coeff = 0.044715

CHIPS = ("x", "y_lo", "z", "y_hi")
EXPERT = ("x", "y_lo", "z")
DP = ("y_hi", "core")


def gelu_tanh(values):
    inner = gelu_coeff * (values + cubic_coeff * values * values * values)
    return 0.5 * values * (1.0 + jnp.tanh(inner))


def gelu_slope(values):
    inner = gelu_coeff * (values + cubic_coeff * values * values * values)
    tangent = jnp.tanh(inner)
    return 0.5 * (1.0 + tangent) + 0.5 * values * (1.0 - tangent * tangent) * gelu_coeff * (
        1.0 + 3.0 * cubic_coeff * values * values
    )


def dot(a, b, dims):
    return lax.dot_general(a, b, (dims, ((), ())), preferred_element_type=jnp.float32)


def swap_cores(values):
    return lax.ppermute(values, "core", [(0, 1), (1, 0)])


def exchange(blocks):
    return lax.all_to_all(blocks, CHIPS, 0, 0, tiled=True)


def shards(tokens, slot_param, up_weight, down_weight, grad_output):
    image_tokens = tokens[0]
    image_grads = grad_output[0]
    up = up_weight[0]
    down = down_weight[0]
    bf16 = jnp.bfloat16
    chips = lax.axis_size(CHIPS)
    slots = slot_param.shape[1]
    width = tokens.shape[2]
    core = lax.axis_index("core")
    param_t = slot_param.T
    logits = dot(param_t, image_tokens, ((1,), (1,)))
    dispatch = jax.nn.softmax(logits, axis=1)
    combine = jax.nn.softmax(logits, axis=0)
    dispatch_b = dispatch.astype(bf16)
    slot_input = dot(dispatch_b, image_tokens, ((1,), (0,))).astype(bf16)
    slot_grad = dot(combine.astype(bf16), image_grads, ((1,), (0,))).astype(bf16)
    rows = jnp.concatenate(
        [slot_input.reshape(slots, 1, 8, 128), slot_grad.reshape(slots, 1, 8, 128)], axis=2
    )
    copies = lax.axis_size("y_hi")
    rows = jnp.broadcast_to(rows, (slots, copies, 16, 128)).reshape(chips, 16, 128)
    mine = exchange(rows)
    both = jnp.concatenate([mine, swap_cores(mine)], axis=0).reshape(2 * chips, 2, width)
    rows_in = both[:, 0]
    rows_grad = both[:, 1]
    preact = dot(rows_in, up, ((1,), (0,)))
    active = gelu_tanh(preact).astype(bf16)
    partial_out = dot(active, down, ((1,), (0,))).astype(bf16)
    grad_active = dot(rows_grad, down, ((1,), (1,)))
    grad_pre = (grad_active * gelu_slope(preact)).astype(bf16)
    partial_in = dot(grad_pre, up, ((1,), (1,))).astype(bf16)
    grad_down = dot(active, rows_grad, ((0,), (0,))).astype(bf16)
    grad_up = dot(rows_in, grad_pre, ((0,), (0,))).astype(bf16)
    partial = jnp.stack([partial_out, partial_in], axis=1).reshape(2, chips, 16, 128)
    summed = partial[0].astype(jnp.float32) + swap_cores(partial[1]).astype(jnp.float32)
    returned = exchange(summed.astype(bf16)).reshape(slots, copies, 2, width)
    returned = jnp.sum(returned.astype(jnp.float32), axis=1).astype(bf16)
    slot_output = returned[:, 0]
    slot_in_grad = returned[:, 1]
    grad_combine = dot(slot_output, image_grads, ((1,), (1,)))
    combine_part = combine * (grad_combine - jnp.sum(combine * grad_combine, axis=0, keepdims=True))
    grad_dispatch = dot(slot_in_grad, image_tokens, ((1,), (1,)))
    dispatch_part = dispatch * (
        grad_dispatch - jnp.sum(dispatch * grad_dispatch, axis=1, keepdims=True)
    )
    grad_logits = (combine_part + dispatch_part).astype(bf16)
    left = jnp.concatenate([dispatch_b, grad_logits], axis=0)
    right = jnp.concatenate([slot_in_grad, param_t], axis=0)
    grad_image = dot(left, right, ((0,), (0,)))
    param_term = dot(grad_logits, image_tokens, ((1,), (0,)))
    halves = param_term.reshape(2, slots // 2, width)
    kept = lax.dynamic_index_in_dim(halves, core, 0, keepdims=False)
    sent = lax.dynamic_index_in_dim(halves, 1 - core, 0, keepdims=False)
    kept = kept + swap_cores(sent)
    blocks = kept.reshape(chips, -1, 128)
    block = jnp.sum(exchange(blocks), axis=0, keepdims=True)
    half = exchange(jnp.broadcast_to(block, blocks.shape)).reshape(1, slots // 2, width)
    other = swap_cores(half)
    first = jnp.where(core == 0, half, other)
    second = jnp.where(core == 0, other, half)
    param_grad = jnp.concatenate([first, second], axis=0).reshape(slots, width).T
    return (grad_image.astype(bf16)[None], param_grad, grad_up[None], grad_down[None])


def solution(mesh):
    devices = mesh.devices.reshape(4, 2, 8, 2, 2)
    cut = Mesh(devices, ("x", "y_lo", "z", "y_hi", "core"))
    return jax.shard_map(
        shards,
        mesh=cut,
        in_specs=(
            P(EXPERT + DP, None, None),
            P(),
            P(EXPERT, None, DP),
            P(EXPERT, DP, None),
            P(EXPERT + DP, None, None),
        ),
        out_specs=(
            P(EXPERT + DP, None, None),
            P(),
            P(EXPERT, None, DP),
            P(EXPERT, DP, None),
        ),
        check_vma=False,
    )
```

```python
import functools

import jax
import jax.numpy as jnp
from jax import lax
from jax.experimental import pallas as pl
from jax.experimental.pallas import tpu as pltpu
from jax.sharding import Mesh, PartitionSpec as P

gelu_coeff = 0.7978845608
cubic_coeff = 0.044715

CHIPS = ("x", "y_lo", "z", "y_hi")
EXPERT = ("x", "y_lo", "z")
DP = ("y_hi", "core")
F32 = jnp.float32
BF16 = jnp.bfloat16
LANES = 128


def dot(a, b, dims):
    return lax.dot_general(a, b, (dims, ((), ())), preferred_element_type=F32)


def swap_cores(values):
    return lax.ppermute(values, "core", [(0, 1), (1, 0)])


def exchange(blocks):
    return lax.all_to_all(blocks, CHIPS, 0, 0, tiled=True)


def call(kernel, outs, scratch=(), flops=0, moved=0, scalars=0, limit=24):
    def run(*args):
        specs = [
            pl.BlockSpec(memory_space=pltpu.SMEM if i < scalars else pltpu.VMEM)
            for i in range(len(args))
        ]
        return pl.pallas_call(
            kernel,
            out_shape=[jax.ShapeDtypeStruct(shape, dtype) for shape, dtype in outs],
            in_specs=specs,
            out_specs=[pl.BlockSpec(memory_space=pltpu.VMEM) for _ in outs],
            scratch_shapes=[pltpu.VMEM(shape, dtype) for shape, dtype in scratch],
            compiler_params=pltpu.CompilerParams(vmem_limit_bytes=limit << 20),
            cost_estimate=pl.CostEstimate(flops=flops, bytes_accessed=moved, transcendentals=0),
        )(*args)

    return run


def to_blocks(scratch, values, first, rows, start=0):
    for k in range(values.shape[1] // LANES):
        scratch[pl.ds(start + first + k, rows, stride=16), :] = values[:, k * LANES : (k + 1) * LANES]


def front_kernel(tokens, grads, param, rows, dispatch, combine, lines):
    slots = param.shape[0]
    logits = dot(param[...], tokens[...], ((1,), (1,)))
    e = jnp.exp(logits - jnp.max(logits, axis=1, keepdims=True))
    d = e / jnp.sum(e, axis=1, keepdims=True)
    e = jnp.exp(logits - jnp.max(logits, axis=0, keepdims=True))
    c = e / jnp.sum(e, axis=0, keepdims=True)
    dispatch[...] = d
    combine[...] = c
    to_blocks(lines, dot(d.astype(BF16), tokens[...], ((1,), (0,))), 0, slots)
    to_blocks(lines, dot(c.astype(BF16), grads[...], ((1,), (0,))), 8, slots)
    blocks = lines[...].reshape(slots, 16, LANES).astype(BF16)
    for copy in range(rows.shape[1]):
        rows[:, copy] = blocks


def expert_kernel(mine, theirs, up, down, own, send, active, grad_pre, rows_in, rows_grad, lines):
    images = mine.shape[0]
    count = 2 * images
    width = up.shape[0]
    hidden = up.shape[1]
    lines[: images * 16, :] = mine[...].reshape(images * 16, LANES).astype(F32)
    lines[images * 16 :, :] = theirs[...].reshape(images * 16, LANES).astype(F32)
    for k in range(8):
        cols = slice(k * LANES, (k + 1) * LANES)
        rows_in[:, cols] = lines[pl.ds(k, count, stride=16), :].astype(BF16)
        rows_grad[:, cols] = lines[pl.ds(8 + k, count, stride=16), :].astype(BF16)
    for c in range(0, hidden, 256):
        cols = slice(c, c + 256)
        v = dot(rows_in[...], up[:, cols], ((1,), (0,)))
        tangent = jnp.tanh(gelu_coeff * (v + cubic_coeff * v * v * v))
        active[:, cols] = (0.5 * v * (1.0 + tangent)).astype(BF16)
        slope = 0.5 * (1.0 + tangent) + 0.5 * v * (1.0 - tangent * tangent) * gelu_coeff * (
            1.0 + 3.0 * cubic_coeff * v * v
        )
        g = dot(rows_grad[...], down[cols, :], ((1,), (1,)))
        grad_pre[:, cols] = (g * slope).astype(BF16)
    for n in range(0, width, 256):
        cols = slice(n, n + 256)
        to_blocks(lines, dot(active[...], down[:, cols], ((1,), (0,))), n // LANES, count)
        to_blocks(lines, dot(grad_pre[...], up[cols, :], ((1,), (1,))), 8 + n // LANES, count)
    own[...] = lines[: images * 16, :].reshape(images, 16, LANES)
    send[...] = lines[images * 16 :, :].reshape(images, 16, LANES).astype(BF16)


def weights_kernel(rows_in, grad_pre, active, rows_grad, grad_up, grad_down):
    grad_up[...] = dot(rows_in[...], grad_pre[...], ((0,), (0,))).astype(BF16)
    grad_down[...] = dot(active[...], rows_grad[...], ((0,), (0,))).astype(BF16)


def weight_grads(rows_in, grad_pre, active, rows_grad):
    count, width = rows_in.shape
    hidden = active.shape[1]
    step = 256
    part = pl.BlockSpec((count, step), lambda i: (0, i))
    whole = lambda n: pl.BlockSpec((count, n), lambda i: (0, 0))
    return pl.pallas_call(
        weights_kernel,
        grid=(width // step,),
        out_shape=[
            jax.ShapeDtypeStruct((width, hidden), BF16),
            jax.ShapeDtypeStruct((hidden, width), BF16),
        ],
        in_specs=[part, whole(hidden), part, whole(width)],
        out_specs=[
            pl.BlockSpec((step, hidden), lambda i: (i, 0)),
            pl.BlockSpec((step, width), lambda i: (i, 0)),
        ],
        compiler_params=pltpu.CompilerParams(vmem_limit_bytes=16 << 20),
        cost_estimate=pl.CostEstimate(
            flops=4 * count * width * hidden, bytes_accessed=4 * width * hidden, transcendentals=0
        ),
    )(rows_in, grad_pre, active, rows_grad)


def back_kernel(core, returned, tokens, grads, dispatch, combine, logit_grads, slot_grads, kept, sent, lines, halves):
    slots = logit_grads.shape[0]
    width = tokens.shape[1]
    total = returned[:, 0].astype(F32)
    for copy in range(1, returned.shape[1]):
        total = total + returned[:, copy].astype(F32)
    lines[...] = total.reshape(slots * 16, LANES)
    outputs = []
    for k in range(8):
        outputs.append(lines[pl.ds(k, slots, stride=16), :].astype(BF16))
        slot_grads[:, k * LANES : (k + 1) * LANES] = lines[pl.ds(8 + k, slots, stride=16), :].astype(BF16)
    c = combine[...]
    g = dot(jnp.concatenate(outputs, axis=1), grads[...], ((1,), (1,)))
    change = c * (g - jnp.sum(c * g, axis=0, keepdims=True))
    d = dispatch[...]
    g = dot(slot_grads[...], tokens[...], ((1,), (1,)))
    change = change + d * (g - jnp.sum(d * g, axis=1, keepdims=True))
    change = change.astype(BF16)
    logit_grads[...] = change
    term = dot(change, tokens[...], ((1,), (0,)))
    for h in range(2):
        for i in range(slots // 16):
            for k in range(width // LANES):
                for a in range(4):
                    row = h * (slots // 2) + i * 8 + a * 2
                    halves[h, (i * (width // LANES) + k) * 4 + a] = term[
                        row : row + 2, k * LANES : (k + 1) * LANES
                    ]
    kept[...] = halves[core[0]]
    sent[...] = halves[1 - core[0]]


def image_kernel(dispatch, logit_grads, slot_grads, param, grad_image):
    left = jnp.concatenate([dispatch[...].astype(BF16), logit_grads[...]], axis=0)
    right = jnp.concatenate([slot_grads[...], param[...]], axis=0)
    grad_image[...] = dot(left, right, ((0,), (0,))).astype(BF16)


def sum_kernel(blocks, out):
    total = jnp.sum(blocks[...], axis=0, keepdims=True)
    out[...] = jnp.broadcast_to(total, out.shape)


def last_kernel(core, half, other, out):
    slots, width = out.shape
    for source, which in ((half, core[0]), (other, 1 - core[0])):
        for i in range(slots // 16):
            for k in range(width // LANES):
                tile = [source[(i * (width // LANES) + k) * 4 + a] for a in range(4)]
                row = pl.multiple_of(which * (slots // 2) + i * 8, 8)
                out[pl.ds(row, 8), k * LANES : (k + 1) * LANES] = jnp.concatenate(tile, axis=0)


def shards(tokens, slot_param, up_weight, down_weight, grad_output):
    image_tokens = tokens[0]
    image_grads = grad_output[0]
    up = up_weight[0]
    down = down_weight[0]
    count, width = image_tokens.shape
    hidden = up.shape[1]
    chips = lax.axis_size(CHIPS)
    copies = lax.axis_size("y_hi")
    slots = slot_param.shape[1]
    core = lax.axis_index("core").astype(jnp.int32).reshape(1)
    param = slot_param.T
    rows, dispatch, combine = call(
        front_kernel,
        [((slots, copies, 16, LANES), BF16), ((slots, count), F32), ((slots, count), F32)],
        [((slots * 16, LANES), F32)],
        flops=6 * slots * count * width,
        moved=6 * count * width,
    )(image_tokens, image_grads, param)
    mine = exchange(rows.reshape(chips, 16, LANES))
    theirs = swap_cores(mine)
    own, send, active, grad_pre, rows_in, rows_grad = call(
        expert_kernel,
        [((chips, 16, LANES), F32), ((chips, 16, LANES), BF16)]
        + [((2 * chips, hidden), BF16)] * 2
        + [((2 * chips, width), BF16)] * 2,
        [((2 * chips * 16, LANES), F32)],
        flops=16 * chips * width * hidden,
        moved=6 * width * hidden,
    )(mine, theirs, up, down)
    summed = (own + swap_cores(send).astype(F32)).astype(BF16)
    returned = exchange(summed)
    grad_up, grad_down = weight_grads(rows_in, grad_pre, active, rows_grad)
    returned, grad_up, grad_down = lax.optimization_barrier((returned, grad_up, grad_down))
    half_shape = (chips, slots * width // 2 // chips // LANES, LANES)
    logit_grads, slot_grads, kept, sent = call(
        back_kernel,
        [((slots, count), BF16), ((slots, width), BF16), (half_shape, F32), (half_shape, F32)],
        [((slots * 16, LANES), F32), ((2,) + half_shape, F32)],
        flops=6 * slots * count * width,
        moved=6 * count * width,
        scalars=1,
    )(core, returned.reshape(slots, copies, 16, LANES), image_tokens, image_grads, dispatch, combine)
    blocks = exchange(kept + swap_cores(sent))
    (grad_image,) = call(
        image_kernel,
        [((count, width), BF16)],
        flops=4 * slots * count * width,
        moved=4 * count * width,
    )(dispatch, logit_grads, slot_grads, param)
    blocks, grad_image = lax.optimization_barrier((blocks, grad_image))
    (block,) = call(sum_kernel, [(half_shape, F32)])(blocks)
    half = exchange(block)
    (param_grad,) = call(last_kernel, [((slots, width), F32)], scalars=1)(core, half, swap_cores(half))
    return (grad_image[None], param_grad.T, grad_up[None], grad_down[None])


def solution(mesh):
    devices = mesh.devices.reshape(4, 2, 8, 2, 2)
    cut = Mesh(devices, ("x", "y_lo", "z", "y_hi", "core"))
    return jax.shard_map(
        shards,
        mesh=cut,
        in_specs=(
            P(EXPERT + DP, None, None),
            P(),
            P(EXPERT, None, DP),
            P(EXPERT, DP, None),
            P(EXPERT + DP, None, None),
        ),
        out_specs=(
            P(EXPERT + DP, None, None),
            P(),
            P(EXPERT, None, DP),
            P(EXPERT, DP, None),
        ),
        check_vma=False,
    )
```

```python
import jax
import jax.numpy as jnp
from jax import lax
from jax.experimental import pallas as pl
from jax.experimental.pallas import tpu as pltpu
from jax.sharding import Mesh, PartitionSpec as P

gelu_coeff = 0.7978845608
cubic_coeff = 0.044715

CHIPS = ("x", "y_lo", "z", "y_hi")
EXPERT = ("x", "y_lo", "z")
DP = ("y_hi", "core")
F32 = jnp.float32
BF16 = jnp.bfloat16
LANES = 128


def dot(a, b, dims):
    return lax.dot_general(a, b, (dims, ((), ())), preferred_element_type=F32)


def swap_cores(values):
    return lax.ppermute(values, "core", [(0, 1), (1, 0)])


def exchange(blocks):
    return lax.all_to_all(blocks, CHIPS, 0, 0, tiled=True)


def call(kernel, outs, scratch=(), flops=0, moved=0, hbm=(), hbm_outs=(), limit=4):
    def shape_of(i, shape, dtype):
        if hbm_outs is None:
            return jax.ShapeDtypeStruct(shape, dtype)
        return pltpu.HBM(shape, dtype) if i in hbm_outs else pltpu.VMEM(shape, dtype)

    kept = () if hbm_outs is None else hbm_outs

    def run(*args):
        args = [pltpu.with_memory_space_constraint(x, pltpu.HBM) if i in hbm else x for i, x in enumerate(args)]
        return pl.pallas_call(
            kernel,
            out_shape=[shape_of(i, shape, dtype) for i, (shape, dtype) in enumerate(outs)],
            in_specs=[pl.BlockSpec(memory_space=pltpu.HBM if i in hbm else pltpu.VMEM) for i in range(len(args))],
            out_specs=[pl.BlockSpec(memory_space=pltpu.HBM if i in kept else pltpu.VMEM) for i in range(len(outs))],
            scratch_shapes=list(scratch),
            compiler_params=pltpu.CompilerParams(vmem_limit_bytes=limit << 20),
            cost_estimate=pl.CostEstimate(flops=flops, bytes_accessed=moved, transcendentals=0),
        )(*args)

    return run


def to_blocks(scratch, values, first, rows, start=0):
    for k in range(values.shape[1] // LANES):
        scratch[pl.ds(start + first + k, rows, stride=16), :] = values[:, k * LANES : (k + 1) * LANES]


PIECES = 4


def front_kernel(tokens_in, grads_in, param_in, up_in, down_in, rows, dispatch, combine, tokens, grads, up, down, param, lines, sems):
    slots, width = param.shape
    count = tokens.shape[0]
    piece = count // PIECES
    copies = [pltpu.make_async_copy(param_in, param, sems.at[2 * PIECES])]
    for j, (source, target) in enumerate(((tokens_in, tokens), (grads_in, grads))):
        for p in range(PIECES):
            part = pl.ds(p * piece, piece)
            copies.append(pltpu.make_async_copy(source.at[part], target.at[part], sems.at[j * PIECES + p]))
    copies.append(pltpu.make_async_copy(up_in, up, sems.at[2 * PIECES + 1]))
    copies.append(pltpu.make_async_copy(down_in, down, sems.at[2 * PIECES + 2]))
    for copy in copies:
        copy.start()
    copies[0].wait()
    logits = []
    for p in range(PIECES):
        copies[1 + p].wait()
        logits.append(dot(param[...], tokens[p * piece : (p + 1) * piece, :], ((1,), (1,))))
    logits = jnp.concatenate(logits, axis=1)
    e = jnp.exp(logits - jnp.max(logits, axis=1, keepdims=True))
    d = e / jnp.sum(e, axis=1, keepdims=True)
    e = jnp.exp(logits - jnp.max(logits, axis=0, keepdims=True))
    c = e / jnp.sum(e, axis=0, keepdims=True)
    dispatch[...] = d
    combine[...] = c
    to_blocks(lines, dot(d.astype(BF16), tokens[...], ((1,), (0,))), 0, slots)
    for p in range(PIECES):
        copies[1 + PIECES + p].wait()
    to_blocks(lines, dot(c.astype(BF16), grads[...], ((1,), (0,))), 8, slots)
    blocks = lines[...].reshape(slots, 16, LANES).astype(BF16)
    for copy in range(rows.shape[1]):
        rows[:, copy] = blocks
    for copy in copies[1 + 2 * PIECES :]:
        copy.wait()


def expert_kernel(mine, up_own, up_other, down_own, down_other, back, keep, swap, parts, lines, sems):
    images = mine.shape[0]
    width, hidden = up_own.shape
    blocks = mine[...]
    parts[0] = blocks[:, :8].reshape(images, width)
    parts[1] = blocks[:, 8:].reshape(images, width)
    targets = [swap.at[j] for j in range(4)] + [keep.at[j] for j in range(2)]
    copies = [pltpu.make_async_copy(parts.at[j], targets[j], sems.at[j]) for j in range(6)]
    copies[0].start()
    copies[1].start()
    rows_in = parts[0]
    rows_grad = parts[1]
    for up, down, first in ((up_other, down_other, 2), (up_own, down_own, 4)):
        for c in range(0, hidden, 256):
            cols = slice(c, c + 256)
            v = dot(rows_in, up[:, cols], ((1,), (0,)))
            tangent = jnp.tanh(gelu_coeff * (v + cubic_coeff * v * v * v))
            parts[first, :, cols] = (0.5 * v * (1.0 + tangent)).astype(BF16)
            slope = 0.5 * (1.0 + tangent) + 0.5 * v * (1.0 - tangent * tangent) * gelu_coeff * (
                1.0 + 3.0 * cubic_coeff * v * v
            )
            g = dot(rows_grad, down[cols, :], ((1,), (1,)))
            parts[first + 1, :, cols] = (g * slope).astype(BF16)
        copies[first].start()
        copies[first + 1].start()
    for n in range(0, width, 256):
        cols = slice(n, n + 256)
        out = dot(parts[4], down_own[:, cols], ((1,), (0,))) + dot(parts[2], down_other[:, cols], ((1,), (0,)))
        to_blocks(lines, out, n // LANES, images)
        out = dot(parts[5], up_own[cols, :], ((1,), (1,))) + dot(parts[3], up_other[cols, :], ((1,), (1,)))
        to_blocks(lines, out, 8 + n // LANES, images)
    back[...] = lines[...].reshape(images, 16, LANES).astype(BF16)
    for copy in copies:
        copy.wait()


def weights_kernel(keep, swap, recv, grad_up, grad_down):
    step = grad_up.shape[0]
    cols = pl.ds(pl.multiple_of(pl.program_id(0) * step, step), step)
    both = lambda a, b: jnp.concatenate([a, b], axis=0)
    rows_in = both(swap[0, :, cols], recv[0, :, cols])
    grad_up[...] = dot(rows_in, both(keep[1], recv[3]), ((0,), (0,))).astype(BF16)
    active = both(keep[0, :, cols], recv[2, :, cols])
    grad_down[...] = dot(active, both(swap[1], recv[1]), ((0,), (0,))).astype(BF16)


def weight_grads(keep, swap, recv):
    images, width = swap.shape[1:]
    step = 256
    whole = lambda n: pl.BlockSpec((n, images, width), lambda i: (0, 0, 0))
    return pl.pallas_call(
        weights_kernel,
        grid=(width // step,),
        out_shape=[jax.ShapeDtypeStruct((width, width), BF16)] * 2,
        in_specs=[whole(2), whole(4), whole(4)],
        out_specs=[pl.BlockSpec((step, width), lambda i: (i, 0))] * 2,
        compiler_params=pltpu.CompilerParams(vmem_limit_bytes=12 << 20),
        cost_estimate=pl.CostEstimate(
            flops=8 * images * width * width, bytes_accessed=4 * width * width, transcendentals=0
        ),
    )(keep, swap, recv)


def back_kernel(returned, tokens, grads, dispatch, combine, logit_grads, slot_grads, blocks, lines):
    slots = logit_grads.shape[0]
    width = tokens.shape[1]
    total = returned[:, 0].astype(F32)
    for copy in range(1, returned.shape[1]):
        total = total + returned[:, copy].astype(F32)
    lines[...] = total.reshape(slots * 16, LANES)
    outputs = []
    for k in range(width // LANES):
        outputs.append(lines[pl.ds(k, slots, stride=16), :].astype(BF16))
        slot_grads[:, k * LANES : (k + 1) * LANES] = lines[pl.ds(8 + k, slots, stride=16), :].astype(BF16)
    c = combine[...]
    g = dot(jnp.concatenate(outputs, axis=1), grads[...], ((1,), (1,)))
    change = c * (g - jnp.sum(c * g, axis=0, keepdims=True))
    d = dispatch[...]
    g = dot(slot_grads[...], tokens[...], ((1,), (1,)))
    change = change + d * (g - jnp.sum(d * g, axis=1, keepdims=True))
    change = change.astype(BF16)
    logit_grads[...] = change
    term = dot(change, tokens[...], ((1,), (0,)))
    for first, row, col in tiles(slots, width):
        blocks[first : first + 16, :] = term[row : row + 16, col : col + LANES].astype(BF16)


def tiles(slots, width):
    first = 0
    for row in range(0, slots, 16):
        for col in range(0, width, LANES):
            yield first, row, col
            first += 16


def image_kernel(dispatch, logit_grads, slot_grads, param, grad_image):
    left = jnp.concatenate([dispatch[...].astype(BF16), logit_grads[...]], axis=0)
    right = jnp.concatenate([slot_grads[...], param[...]], axis=0)
    grad_image[...] = dot(left, right, ((0,), (0,))).astype(BF16)


def add_kernel(a, b, out):
    out[...] = a[...] + b[...]


def sum_kernel(blocks, out):
    rows = out.shape[0]
    total = jnp.sum(blocks[...].astype(F32).reshape(-1, 8, LANES), axis=0)
    out[...] = sum(total[i : i + rows] for i in range(0, 8, rows))


def spread_kernel(a, b, out):
    total = a[...] + b[...]
    tile = jnp.concatenate([total] * (16 // total.shape[0]), axis=0).astype(BF16)
    for first in range(0, out.shape[0], 16):
        out[first : first + 16, :] = tile


def last_kernel(blocks, out):
    for first, row, col in tiles(*out.shape):
        out[row : row + 16, col : col + LANES] = blocks[first : first + 16, :].astype(F32)


def shards(tokens, slot_param, up_weight, down_weight, grad_output):
    image_tokens = tokens[0]
    image_grads = grad_output[0]
    up = up_weight[0]
    down = down_weight[0]
    count, width = image_tokens.shape
    hidden = up.shape[1]
    chips = lax.axis_size(CHIPS)
    copies = lax.axis_size("y_hi")
    slots = slot_param.shape[1]
    param = slot_param.T
    up_other = swap_cores(up)
    down_other = swap_cores(down)
    rows, dispatch, combine, image_tokens, image_grads, up_own, down_own = call(
        front_kernel,
        [((slots, copies, 16, LANES), BF16), ((slots, count), F32), ((slots, count), F32)]
        + [((count, width), BF16)] * 2
        + [((width, hidden), BF16), ((hidden, width), BF16)],
        [
            pltpu.VMEM((slots, width), BF16),
            pltpu.VMEM((slots * 16, LANES), F32),
            pltpu.SemaphoreType.DMA((2 * PIECES + 3,)),
        ],
        flops=6 * slots * count * width,
        moved=16 * width * hidden,
        hbm=(0, 1, 2, 3, 4),
    )(image_tokens, image_grads, param, up, down)
    mine = exchange(rows.reshape(chips, 16, LANES))
    back, keep, swap = call(
        expert_kernel,
        [((chips, 16, LANES), BF16), ((2, chips, width), BF16), ((4, chips, width), BF16)],
        [
            pltpu.VMEM((6, chips, width), BF16),
            pltpu.VMEM((chips * 16, LANES), F32),
            pltpu.SemaphoreType.DMA((6,)),
        ],
        flops=16 * chips * width * hidden,
        moved=4 * width * hidden,
        hbm_outs=(1, 2),
        limit=8,
    )(mine, up_own, up_other, down_own, down_other)
    returned = exchange(back)
    lines = slots * width // LANES
    logit_grads, slot_grads, blocks = call(
        back_kernel,
        [((slots, count), BF16), ((slots, width), BF16), ((lines, LANES), BF16)],
        [pltpu.VMEM((slots * 16, LANES), F32)],
        flops=6 * slots * count * width,
        moved=6 * count * width,
    )(returned.reshape(slots, copies, 16, LANES), image_tokens, image_grads, dispatch, combine)
    blocks = exchange(blocks.reshape(chips, lines // chips, LANES)).reshape(lines, LANES)
    (block,) = call(sum_kernel, [((lines // chips, LANES), F32)])(blocks)
    block, other, keep, swap, logit_grads, slot_grads = lax.optimization_barrier(
        (block, swap_cores(block), keep, swap, logit_grads, slot_grads)
    )
    recv = swap_cores(swap)
    (blocks,) = call(spread_kernel, [((lines, LANES), BF16)])(block, other)
    blocks = exchange(blocks.reshape(chips, lines // chips, LANES)).reshape(lines, LANES)
    grad_up, grad_down = weight_grads(keep, swap, recv)
    (grad_image,) = call(
        image_kernel,
        [((count, width), BF16)],
        flops=4 * slots * count * width,
        moved=4 * count * width,
        hbm_outs=None,
    )(dispatch, logit_grads, slot_grads, param)
    blocks, grad_image, grad_up, grad_down = lax.optimization_barrier((blocks, grad_image, grad_up, grad_down))
    (param_grad,) = call(last_kernel, [((slots, width), F32)], hbm_outs=None)(blocks)
    return (grad_image[None], param_grad.T, grad_up[None], grad_down[None])


def solution(mesh):
    devices = mesh.devices.reshape(4, 2, 8, 2, 2)
    cut = Mesh(devices, ("x", "y_lo", "z", "y_hi", "core"))
    return jax.shard_map(
        shards,
        mesh=cut,
        in_specs=(
            P(EXPERT + DP, None, None),
            P(),
            P(EXPERT, None, DP),
            P(EXPERT, DP, None),
            P(EXPERT + DP, None, None),
        ),
        out_specs=(
            P(EXPERT + DP, None, None),
            P(),
            P(EXPERT, None, DP),
            P(EXPERT, DP, None),
        ),
        check_vma=False,
    )
```

```python
import jax
import jax.numpy as jnp
from jax import lax
from jax.experimental import pallas as pl
from jax.experimental.pallas import tpu as pltpu
from jax.sharding import Mesh, PartitionSpec as P

gelu_coeff = 0.7978845608
cubic_coeff = 0.044715

CUT = {"x": 4, "y_lo": 2, "z": 8, "y_hi": 2, "core": 2}
CHIPS = ("y_hi", "y_lo", "z", "x")
EXPERT = ("x", "y_lo", "z")
DP = ("y_hi", "core")
PLANE = ("x", "y_lo", "y_hi", "core")
F32 = jnp.float32
BF16 = jnp.bfloat16
LANES = 128


def dot(a, b, dims):
    return lax.dot_general(a, b, (dims, ((), ())), preferred_element_type=F32)


def swap_cores(values):
    return lax.ppermute(values, "core", [(0, 1), (1, 0)])


def exchange(blocks, axes=CHIPS):
    return lax.all_to_all(blocks, axes, 0, 0, tiled=True)


def call(kernel, outs, scratch=(), flops=0, moved=0, hbm=(), hbm_outs=(), limit=4):
    def shape_of(i, shape, dtype):
        if hbm_outs is None:
            return jax.ShapeDtypeStruct(shape, dtype)
        return pltpu.HBM(shape, dtype) if i in hbm_outs else pltpu.VMEM(shape, dtype)

    kept = () if hbm_outs is None else hbm_outs

    def run(*args):
        args = [pltpu.with_memory_space_constraint(x, pltpu.HBM) if i in hbm else x for i, x in enumerate(args)]
        return pl.pallas_call(
            kernel,
            out_shape=[shape_of(i, shape, dtype) for i, (shape, dtype) in enumerate(outs)],
            in_specs=[pl.BlockSpec(memory_space=pltpu.HBM if i in hbm else pltpu.VMEM) for i in range(len(args))],
            out_specs=[pl.BlockSpec(memory_space=pltpu.HBM if i in kept else pltpu.VMEM) for i in range(len(outs))],
            scratch_shapes=list(scratch),
            compiler_params=pltpu.CompilerParams(vmem_limit_bytes=limit << 20),
            cost_estimate=pl.CostEstimate(flops=flops, bytes_accessed=moved, transcendentals=0),
        )(*args)

    return run


def blocks_of(slot):
    place = {}
    for axis in reversed(EXPERT):
        slot, place[axis] = divmod(slot, CUT[axis])
    found = []
    for place["y_hi"] in range(CUT["y_hi"]):
        block = 0
        for axis in CHIPS:
            block = block * CUT[axis] + place[axis]
        found.append(block)
    return found


def to_blocks(scratch, values, first, rows, start=0):
    for k in range(values.shape[1] // LANES):
        scratch[pl.ds(start + first + k, rows, stride=16), :] = values[:, k * LANES : (k + 1) * LANES]


PIECES = 4


def front_kernel(tokens_in, grads_in, param_in, up_in, down_in, rows, dispatch, combine, tokens, grads, up, down, param, lines, sems):
    slots, width = param.shape
    count = tokens.shape[0]
    piece = count // PIECES
    copies = [pltpu.make_async_copy(param_in, param, sems.at[2 * PIECES])]
    for j, (source, target) in enumerate(((tokens_in, tokens), (grads_in, grads))):
        for p in range(PIECES):
            part = pl.ds(p * piece, piece)
            copies.append(pltpu.make_async_copy(source.at[part], target.at[part], sems.at[j * PIECES + p]))
    copies.append(pltpu.make_async_copy(up_in, up, sems.at[2 * PIECES + 1]))
    copies.append(pltpu.make_async_copy(down_in, down, sems.at[2 * PIECES + 2]))
    for copy in copies:
        copy.start()
    copies[0].wait()
    logits = []
    for p in range(PIECES):
        copies[1 + p].wait()
        logits.append(dot(param[...], tokens[p * piece : (p + 1) * piece, :], ((1,), (1,))))
    logits = jnp.concatenate(logits, axis=1)
    e = jnp.exp(logits - jnp.max(logits, axis=1, keepdims=True))
    d = e / jnp.sum(e, axis=1, keepdims=True)
    e = jnp.exp(logits - jnp.max(logits, axis=0, keepdims=True))
    c = e / jnp.sum(e, axis=0, keepdims=True)
    dispatch[...] = d
    combine[...] = c
    to_blocks(lines, dot(d.astype(BF16), tokens[...], ((1,), (0,))), 0, slots)
    for p in range(PIECES):
        copies[1 + PIECES + p].wait()
    to_blocks(lines, dot(c.astype(BF16), grads[...], ((1,), (0,))), 8, slots)
    for slot in range(slots):
        for block in blocks_of(slot):
            rows[block] = lines[slot * 16 : slot * 16 + 16, :].astype(BF16)
    for copy in copies[1 + 2 * PIECES :]:
        copy.wait()


def expert_kernel(mine, up_own, up_other, down_own, down_other, back, keep, swap, parts, lines, sems):
    images = mine.shape[0]
    width, hidden = up_own.shape
    blocks = mine[...]
    parts[0] = blocks[:, :8].reshape(images, width)
    parts[1] = blocks[:, 8:].reshape(images, width)
    targets = [swap.at[j] for j in range(4)] + [keep.at[j] for j in range(2)]
    copies = [pltpu.make_async_copy(parts.at[j], targets[j], sems.at[j]) for j in range(6)]
    copies[0].start()
    copies[1].start()
    rows_in = parts[0]
    rows_grad = parts[1]
    for up, down, first in ((up_other, down_other, 2), (up_own, down_own, 4)):
        for c in range(0, hidden, 256):
            cols = slice(c, c + 256)
            v = dot(rows_in, up[:, cols], ((1,), (0,)))
            tangent = jnp.tanh(gelu_coeff * (v + cubic_coeff * v * v * v))
            parts[first, :, cols] = (0.5 * v * (1.0 + tangent)).astype(BF16)
            slope = 0.5 * (1.0 + tangent) + 0.5 * v * (1.0 - tangent * tangent) * gelu_coeff * (
                1.0 + 3.0 * cubic_coeff * v * v
            )
            g = dot(rows_grad, down[cols, :], ((1,), (1,)))
            parts[first + 1, :, cols] = (g * slope).astype(BF16)
        copies[first].start()
        copies[first + 1].start()
    for n in range(0, width, 256):
        cols = slice(n, n + 256)
        out = dot(parts[4], down_own[:, cols], ((1,), (0,))) + dot(parts[2], down_other[:, cols], ((1,), (0,)))
        to_blocks(lines, out, n // LANES, images)
        out = dot(parts[5], up_own[cols, :], ((1,), (1,))) + dot(parts[3], up_other[cols, :], ((1,), (1,)))
        to_blocks(lines, out, 8 + n // LANES, images)
    back[...] = lines[...].reshape(images, 16, LANES).astype(BF16)
    for copy in copies:
        copy.wait()


def weights_kernel(keep, swap, recv, grad_up, grad_down):
    step = grad_up.shape[0]
    cols = pl.ds(pl.multiple_of(pl.program_id(0) * step, step), step)
    both = lambda a, b: jnp.concatenate([a, b], axis=0)
    rows_in = both(swap[0, :, cols], recv[0, :, cols])
    grad_up[...] = dot(rows_in, both(keep[1], recv[3]), ((0,), (0,))).astype(BF16)
    active = both(keep[0, :, cols], recv[2, :, cols])
    grad_down[...] = dot(active, both(swap[1], recv[1]), ((0,), (0,))).astype(BF16)


def weight_grads(keep, swap, recv):
    images, width = swap.shape[1:]
    step = 256
    whole = lambda n: pl.BlockSpec((n, images, width), lambda i: (0, 0, 0))
    return pl.pallas_call(
        weights_kernel,
        grid=(width // step,),
        out_shape=[jax.ShapeDtypeStruct((width, width), BF16)] * 2,
        in_specs=[whole(2), whole(4), whole(4)],
        out_specs=[pl.BlockSpec((step, width), lambda i: (i, 0))] * 2,
        compiler_params=pltpu.CompilerParams(vmem_limit_bytes=12 << 20),
        cost_estimate=pl.CostEstimate(
            flops=8 * images * width * width, bytes_accessed=4 * width * width, transcendentals=0
        ),
    )(keep, swap, recv)


def back_kernel(returned, tokens, grads, dispatch, combine, logit_grads, slot_grads, blocks, lines):
    slots = logit_grads.shape[0]
    width = tokens.shape[1]
    for slot in range(slots):
        lines[slot * 16 : slot * 16 + 16, :] = sum(returned[block].astype(F32) for block in blocks_of(slot))
    outputs = []
    for k in range(width // LANES):
        outputs.append(lines[pl.ds(k, slots, stride=16), :].astype(BF16))
        slot_grads[:, k * LANES : (k + 1) * LANES] = lines[pl.ds(8 + k, slots, stride=16), :].astype(BF16)
    c = combine[...]
    g = dot(jnp.concatenate(outputs, axis=1), grads[...], ((1,), (1,)))
    change = c * (g - jnp.sum(c * g, axis=0, keepdims=True))
    d = dispatch[...]
    g = dot(slot_grads[...], tokens[...], ((1,), (1,)))
    change = change + d * (g - jnp.sum(d * g, axis=1, keepdims=True))
    change = change.astype(BF16)
    logit_grads[...] = change
    term = dot(change, tokens[...], ((1,), (0,)))
    for first, row, col in tiles(slots, width):
        blocks[first : first + 16, :] = term[row : row + 16, col : col + LANES].astype(BF16)


def tiles(slots, width):
    first = 0
    for row in range(0, slots, 16):
        for col in range(0, width, LANES):
            yield first, row, col
            first += 16


def image_kernel(dispatch, logit_grads, slot_grads, param, grad_image):
    left = jnp.concatenate([dispatch[...].astype(BF16), logit_grads[...]], axis=0)
    right = jnp.concatenate([slot_grads[...], param[...]], axis=0)
    grad_image[...] = dot(left, right, ((0,), (0,))).astype(BF16)


def add_kernel(a, b, out):
    out[...] = a[...] + b[...]


def sum_kernel(blocks, out):
    total = jnp.sum(blocks[...].astype(F32), axis=0)
    out[...] = jnp.broadcast_to(total.astype(out.dtype)[None], out.shape)


def last_kernel(blocks, out):
    for first, row, col in tiles(*out.shape):
        out[row : row + 16, col : col + LANES] = blocks[first : first + 16, :].astype(F32)


def shards(tokens, slot_param, up_weight, down_weight, grad_output):
    image_tokens = tokens[0]
    image_grads = grad_output[0]
    up = up_weight[0]
    down = down_weight[0]
    count, width = image_tokens.shape
    hidden = up.shape[1]
    chips = lax.axis_size(CHIPS)
    slots = slot_param.shape[1]
    param = slot_param.T
    up_other = swap_cores(up)
    down_other = swap_cores(down)
    rows, dispatch, combine, image_tokens, image_grads, up_own, down_own = call(
        front_kernel,
        [((chips, 16, LANES), BF16), ((slots, count), F32), ((slots, count), F32)]
        + [((count, width), BF16)] * 2
        + [((width, hidden), BF16), ((hidden, width), BF16)],
        [
            pltpu.VMEM((slots, width), BF16),
            pltpu.VMEM((slots * 16, LANES), F32),
            pltpu.SemaphoreType.DMA((2 * PIECES + 3,)),
        ],
        flops=6 * slots * count * width,
        moved=16 * width * hidden,
        hbm=(0, 1, 2, 3, 4),
    )(image_tokens, image_grads, param, up, down)
    mine = exchange(rows)
    back, keep, swap = call(
        expert_kernel,
        [((chips, 16, LANES), BF16), ((2, chips, width), BF16), ((4, chips, width), BF16)],
        [
            pltpu.VMEM((6, chips, width), BF16),
            pltpu.VMEM((chips * 16, LANES), F32),
            pltpu.SemaphoreType.DMA((6,)),
        ],
        flops=16 * chips * width * hidden,
        moved=4 * width * hidden,
        hbm_outs=(1, 2),
        limit=8,
    )(mine, up_own, up_other, down_own, down_other)
    returned = exchange(back)
    lines = slots * width // LANES
    logit_grads, slot_grads, blocks = call(
        back_kernel,
        [((slots, count), BF16), ((slots, width), BF16), ((lines, LANES), BF16)],
        [pltpu.VMEM((slots * 16, LANES), F32)],
        flops=6 * slots * count * width,
        moved=6 * count * width,
    )(returned, image_tokens, image_grads, dispatch, combine)
    plane = lax.axis_size(PLANE)
    depth = lax.axis_size("z")
    blocks = exchange(blocks.reshape(plane, lines // plane, LANES), PLANE)
    (blocks,) = call(sum_kernel, [((depth, lines // plane, LANES), F32)])(blocks)
    blocks = exchange(blocks, "z")
    blocks, keep, swap, logit_grads, slot_grads = lax.optimization_barrier(
        (blocks, keep, swap, logit_grads, slot_grads)
    )
    recv = swap_cores(swap)
    (blocks,) = call(sum_kernel, [((plane, lines // plane, LANES), BF16)])(blocks)
    blocks = exchange(blocks, PLANE).reshape(lines, LANES)
    grad_up, grad_down = weight_grads(keep, swap, recv)
    (grad_image,) = call(
        image_kernel,
        [((count, width), BF16)],
        flops=4 * slots * count * width,
        moved=4 * count * width,
        hbm_outs=None,
    )(dispatch, logit_grads, slot_grads, param)
    blocks, grad_image, grad_up, grad_down = lax.optimization_barrier((blocks, grad_image, grad_up, grad_down))
    (param_grad,) = call(last_kernel, [((slots, width), F32)], hbm_outs=None)(blocks)
    return (grad_image[None], param_grad.T, grad_up[None], grad_down[None])


def solution(mesh):
    cut = Mesh(mesh.devices.reshape(tuple(CUT.values())), tuple(CUT))
    return jax.shard_map(
        shards,
        mesh=cut,
        in_specs=(
            P(EXPERT + DP, None, None),
            P(),
            P(EXPERT, None, DP),
            P(EXPERT, DP, None),
            P(EXPERT + DP, None, None),
        ),
        out_specs=(
            P(EXPERT + DP, None, None),
            P(),
            P(EXPERT, None, DP),
            P(EXPERT, DP, None),
        ),
        check_vma=False,
    )
```

```python
import jax
import jax.numpy as jnp
from jax import lax
from jax.experimental import pallas as pl
from jax.experimental.pallas import tpu as pltpu
from jax.sharding import Mesh, PartitionSpec as P

gelu_coeff = 0.7978845608
cubic_coeff = 0.044715

CUT = {"x": 4, "y_lo": 2, "z": 8, "y_hi": 2, "core": 2}
CHIPS = ("y_hi", "y_lo", "z", "x")
EXPERT = ("x", "y_lo", "z")
DP = ("y_hi", "core")
PLANE = ("x", "y_lo", "y_hi", "core")
F32 = jnp.float32
BF16 = jnp.bfloat16
LANES = 128


def dot(a, b, dims):
    return lax.dot_general(a, b, (dims, ((), ())), preferred_element_type=F32)


def swap_cores(values):
    return lax.ppermute(values, "core", [(0, 1), (1, 0)])


def exchange(blocks, axes=CHIPS):
    return lax.all_to_all(blocks, axes, 0, 0, tiled=True)


def call(kernel, outs, scratch=(), flops=0, moved=0, hbm=(), hbm_outs=(), limit=4):
    def shape_of(i, shape, dtype):
        if hbm_outs is None:
            return jax.ShapeDtypeStruct(shape, dtype)
        return pltpu.HBM(shape, dtype) if i in hbm_outs else pltpu.VMEM(shape, dtype)

    kept = () if hbm_outs is None else hbm_outs

    def run(*args):
        args = [pltpu.with_memory_space_constraint(x, pltpu.HBM) if i in hbm else x for i, x in enumerate(args)]
        return pl.pallas_call(
            kernel,
            out_shape=[shape_of(i, shape, dtype) for i, (shape, dtype) in enumerate(outs)],
            in_specs=[pl.BlockSpec(memory_space=pltpu.HBM if i in hbm else pltpu.VMEM) for i in range(len(args))],
            out_specs=[pl.BlockSpec(memory_space=pltpu.HBM if i in kept else pltpu.VMEM) for i in range(len(outs))],
            scratch_shapes=list(scratch),
            compiler_params=pltpu.CompilerParams(vmem_limit_bytes=limit << 20),
            cost_estimate=pl.CostEstimate(flops=flops, bytes_accessed=moved, transcendentals=0),
        )(*args)

    return run


def blocks_of(slot):
    place = {}
    for axis in reversed(EXPERT):
        slot, place[axis] = divmod(slot, CUT[axis])
    found = []
    for place["y_hi"] in range(CUT["y_hi"]):
        block = 0
        for axis in CHIPS:
            block = block * CUT[axis] + place[axis]
        found.append(block)
    return found


def to_blocks(scratch, values, first, rows, start=0):
    for k in range(values.shape[1] // LANES):
        scratch[pl.ds(start + first + k, rows, stride=16), :] = values[:, k * LANES : (k + 1) * LANES]


PIECES = 4


def front_kernel(tokens_in, grads_in, param_in, up_in, down_in, rows, dispatch, combine, tokens, grads, up, down, param, lines, sems):
    slots, width = param.shape
    count = tokens.shape[0]
    piece = count // PIECES
    copies = [pltpu.make_async_copy(param_in, param, sems.at[2 * PIECES])]
    for j, (source, target) in enumerate(((tokens_in, tokens), (grads_in, grads))):
        for p in range(PIECES):
            part = pl.ds(p * piece, piece)
            copies.append(pltpu.make_async_copy(source.at[part], target.at[part], sems.at[j * PIECES + p]))
    copies.append(pltpu.make_async_copy(up_in, up, sems.at[2 * PIECES + 1]))
    copies.append(pltpu.make_async_copy(down_in, down, sems.at[2 * PIECES + 2]))
    for copy in copies:
        copy.start()
    copies[0].wait()
    for p in range(PIECES):
        copies[1 + p].wait()
    logits = dot(param[...], tokens[...], ((1,), (1,)))
    e = jnp.exp(logits - jnp.max(logits, axis=1, keepdims=True))
    d = e / jnp.sum(e, axis=1, keepdims=True)
    e = jnp.exp(logits - jnp.max(logits, axis=0, keepdims=True))
    c = e / jnp.sum(e, axis=0, keepdims=True)
    dispatch[...] = d
    combine[...] = c
    to_blocks(lines, dot(d.astype(BF16), tokens[...], ((1,), (0,))), 0, slots)
    for p in range(PIECES):
        copies[1 + PIECES + p].wait()
    to_blocks(lines, dot(c.astype(BF16), grads[...], ((1,), (0,))), 8, slots)
    for slot in range(slots):
        for block in blocks_of(slot):
            rows[block] = lines[slot * 16 : slot * 16 + 16, :].astype(BF16)
    for copy in copies[1 + 2 * PIECES :]:
        copy.wait()


def expert_kernel(mine, up_own, up_other, down_own, down_other, back, keep, swap, parts, lines, sems):
    images = mine.shape[0]
    width, hidden = up_own.shape
    blocks = mine[...]
    parts[0] = blocks[:, :8].reshape(images, width)
    parts[1] = blocks[:, 8:].reshape(images, width)
    copies = [
        pltpu.make_async_copy(parts.at[pl.ds(0, 4)], swap, sems.at[0]),
        pltpu.make_async_copy(parts.at[pl.ds(4, 2)], keep, sems.at[1]),
    ]
    rows_in = parts[0]
    rows_grad = parts[1]
    for up, down, first in ((up_other, down_other, 2), (up_own, down_own, 4)):
        for c in range(0, hidden, 256):
            cols = slice(c, c + 256)
            v = dot(rows_in, up[:, cols], ((1,), (0,)))
            tangent = jnp.tanh(gelu_coeff * (v + cubic_coeff * v * v * v))
            parts[first, :, cols] = (0.5 * v * (1.0 + tangent)).astype(BF16)
            slope = 0.5 * (1.0 + tangent) + 0.5 * v * (1.0 - tangent * tangent) * gelu_coeff * (
                1.0 + 3.0 * cubic_coeff * v * v
            )
            g = dot(rows_grad, down[cols, :], ((1,), (1,)))
            parts[first + 1, :, cols] = (g * slope).astype(BF16)
        copies[first // 2 - 1].start()
    for n in range(0, width, 256):
        cols = slice(n, n + 256)
        out = dot(parts[4], down_own[:, cols], ((1,), (0,))) + dot(parts[2], down_other[:, cols], ((1,), (0,)))
        to_blocks(lines, out, n // LANES, images)
        out = dot(parts[5], up_own[cols, :], ((1,), (1,))) + dot(parts[3], up_other[cols, :], ((1,), (1,)))
        to_blocks(lines, out, 8 + n // LANES, images)
    back[...] = lines[: images * 16, :].reshape(images, 16, LANES).astype(BF16)
    for copy in copies:
        copy.wait()


def weights_kernel(keep, swap, recv, grad_up, grad_down):
    step = grad_up.shape[0]
    cols = pl.ds(pl.multiple_of(pl.program_id(0) * step, step), step)
    both = lambda a, b: jnp.concatenate([a, b], axis=0)
    rows_in = both(swap[0, :, cols], recv[0, :, cols])
    grad_up[...] = dot(rows_in, both(keep[1], recv[3]), ((0,), (0,))).astype(BF16)
    active = both(keep[0, :, cols], recv[2, :, cols])
    grad_down[...] = dot(active, both(swap[1], recv[1]), ((0,), (0,))).astype(BF16)


def weight_grads(keep, swap, recv):
    images, width = swap.shape[1:]
    step = 256
    whole = lambda n: pl.BlockSpec((n, images, width), lambda i: (0, 0, 0))
    return pl.pallas_call(
        weights_kernel,
        grid=(width // step,),
        out_shape=[jax.ShapeDtypeStruct((width, width), BF16)] * 2,
        in_specs=[whole(2), whole(4), whole(4)],
        out_specs=[pl.BlockSpec((step, width), lambda i: (i, 0))] * 2,
        compiler_params=pltpu.CompilerParams(vmem_limit_bytes=12 << 20),
        cost_estimate=pl.CostEstimate(
            flops=8 * images * width * width, bytes_accessed=4 * width * width, transcendentals=0
        ),
    )(keep, swap, recv)


def back_kernel(returned, tokens, grads, dispatch, combine, logit_grads, slot_grads, blocks, lines):
    slots = logit_grads.shape[0]
    width = tokens.shape[1]
    for slot in range(slots):
        lines[slot * 16 : slot * 16 + 16, :] = sum(returned[block].astype(F32) for block in blocks_of(slot))
    outputs = []
    for k in range(width // LANES):
        outputs.append(lines[pl.ds(k, slots, stride=16), :].astype(BF16))
        slot_grads[:, k * LANES : (k + 1) * LANES] = lines[pl.ds(8 + k, slots, stride=16), :].astype(BF16)
    c = combine[...]
    g = dot(jnp.concatenate(outputs, axis=1), grads[...], ((1,), (1,)))
    change = c * (g - jnp.sum(c * g, axis=0, keepdims=True))
    d = dispatch[...]
    g = dot(slot_grads[...], tokens[...], ((1,), (1,)))
    change = change + d * (g - jnp.sum(d * g, axis=1, keepdims=True))
    change = change.astype(BF16)
    logit_grads[...] = change
    term = dot(change, tokens[...], ((1,), (0,)))
    for first, row, col in tiles(slots, width):
        blocks[first : first + 16, :] = term[row : row + 16, col : col + LANES].astype(BF16)


def tiles(slots, width):
    first = 0
    for row in range(0, slots, 16):
        for col in range(0, width, LANES):
            yield first, row, col
            first += 16


def image_kernel(dispatch, logit_grads, slot_grads, param, grad_image):
    left = jnp.concatenate([dispatch[...].astype(BF16), logit_grads[...]], axis=0)
    right = jnp.concatenate([slot_grads[...], param[...]], axis=0)
    grad_image[...] = dot(left, right, ((0,), (0,))).astype(BF16)


def add_kernel(a, b, out):
    out[...] = a[...] + b[...]


def sum_kernel(blocks, out):
    total = jnp.sum(blocks[...].astype(F32), axis=0)
    out[...] = jnp.broadcast_to(total.astype(out.dtype)[None], out.shape)


def last_kernel(blocks, out):
    for first, row, col in tiles(*out.shape):
        out[row : row + 16, col : col + LANES] = blocks[first : first + 16, :].astype(F32)


def shards(tokens, slot_param, up_weight, down_weight, grad_output):
    image_tokens = tokens[0]
    image_grads = grad_output[0]
    up = up_weight[0]
    down = down_weight[0]
    count, width = image_tokens.shape
    hidden = up.shape[1]
    chips = lax.axis_size(CHIPS)
    slots = slot_param.shape[1]
    param = slot_param.T
    up_other = swap_cores(up)
    down_other = swap_cores(down)
    rows, dispatch, combine, image_tokens, image_grads, up_own, down_own = call(
        front_kernel,
        [((chips, 16, LANES), BF16), ((slots, count), F32), ((slots, count), F32)]
        + [((count, width), BF16)] * 2
        + [((width, hidden), BF16), ((hidden, width), BF16)],
        [
            pltpu.VMEM((slots, width), BF16),
            pltpu.VMEM((slots * 16 + 16, LANES), F32),
            pltpu.SemaphoreType.DMA((2 * PIECES + 3,)),
        ],
        flops=6 * slots * count * width,
        moved=16 * width * hidden,
        hbm=(0, 1, 2, 3, 4),
    )(image_tokens, image_grads, param, up, down)
    mine = exchange(rows)
    back, keep, swap = call(
        expert_kernel,
        [((chips, 16, LANES), BF16), ((2, chips, width), BF16), ((4, chips, width), BF16)],
        [
            pltpu.VMEM((6, chips, width), BF16),
            pltpu.VMEM((chips * 16 + 16, LANES), F32),
            pltpu.SemaphoreType.DMA((2,)),
        ],
        flops=16 * chips * width * hidden,
        moved=4 * width * hidden,
        hbm_outs=(1, 2),
        limit=8,
    )(mine, up_own, up_other, down_own, down_other)
    returned = exchange(back)
    lines = slots * width // LANES
    logit_grads, slot_grads, blocks = call(
        back_kernel,
        [((slots, count), BF16), ((slots, width), BF16), ((lines, LANES), BF16)],
        [pltpu.VMEM((slots * 16 + 16, LANES), F32)],
        flops=6 * slots * count * width,
        moved=6 * count * width,
    )(returned, image_tokens, image_grads, dispatch, combine)
    plane = lax.axis_size(PLANE)
    depth = lax.axis_size("z")
    blocks = exchange(blocks.reshape(plane, lines // plane, LANES), PLANE)
    (blocks,) = call(sum_kernel, [((depth, lines // plane, LANES), F32)])(blocks)
    blocks = exchange(blocks, "z")
    blocks, keep, swap, logit_grads, slot_grads = lax.optimization_barrier(
        (blocks, keep, swap, logit_grads, slot_grads)
    )
    recv = swap_cores(swap)
    (blocks,) = call(sum_kernel, [((plane, lines // plane, LANES), BF16)])(blocks)
    blocks = exchange(blocks, PLANE).reshape(lines, LANES)
    grad_up, grad_down = weight_grads(keep, swap, recv)
    (grad_image,) = call(
        image_kernel,
        [((count, width), BF16)],
        flops=4 * slots * count * width,
        moved=4 * count * width,
        hbm_outs=None,
    )(dispatch, logit_grads, slot_grads, param)
    blocks, grad_image, grad_up, grad_down = lax.optimization_barrier((blocks, grad_image, grad_up, grad_down))
    (param_grad,) = call(last_kernel, [((slots, width), F32)], hbm_outs=None)(blocks)
    return (grad_image[None], param_grad.T, grad_up[None], grad_down[None])


def solution(mesh):
    cut = Mesh(mesh.devices.reshape(tuple(CUT.values())), tuple(CUT))
    return jax.shard_map(
        shards,
        mesh=cut,
        in_specs=(
            P(EXPERT + DP, None, None),
            P(),
            P(EXPERT, None, DP),
            P(EXPERT, DP, None),
            P(EXPERT + DP, None, None),
        ),
        out_specs=(
            P(EXPERT + DP, None, None),
            P(),
            P(EXPERT, None, DP),
            P(EXPERT, DP, None),
        ),
        check_vma=False,
    )
```

```python
import math

import jax
import jax.numpy as jnp
import numpy as np
from jax import lax
from jax.experimental import pallas as pl
from jax.experimental.pallas import tpu as pltpu
from jax.sharding import Mesh, PartitionSpec as P

gelu_coeff = 0.7978845608
cubic_coeff = 0.044715

CUT = {"x": 4, "y_lo": 2, "z": 8, "y_hi": 2, "core": 2}
CHIPS = ("y_hi", "y_lo", "z", "x")
ROOT = {"x": 2, "y_lo": 0, "z": 6, "y_hi": 1}
EXPERT = ("x", "y_lo", "z")
DP = ("y_hi", "core")
PLANE = ("x", "y_lo", "y_hi", "core")
F32 = jnp.float32
BF16 = jnp.bfloat16
LANES = 128


def dot(a, b, dims):
    return lax.dot_general(a, b, (dims, ((), ())), preferred_element_type=F32)


def swap_cores(values):
    return lax.ppermute(values, "core", [(0, 1), (1, 0)])


def exchange(blocks, axes):
    numbers = np.arange(math.prod(CUT.values())).reshape(tuple(CUT.values()))
    for axis, first in ROOT.items():
        numbers = np.roll(numbers, -first, axis=list(CUT).index(axis))
    order = [axis for axis in CUT if axis not in axes] + list(axes)
    numbers = numbers.transpose([list(CUT).index(axis) for axis in order])
    groups = numbers.reshape(-1, math.prod(CUT[axis] for axis in axes)).tolist()
    return lax.all_to_all(blocks, tuple(CUT), 0, 0, axis_index_groups=groups, tiled=True)


def call(kernel, outs, scratch=(), flops=0, moved=0, hbm=(), hbm_outs=(), limit=4):
    def shape_of(i, shape, dtype):
        if hbm_outs is None:
            return jax.ShapeDtypeStruct(shape, dtype)
        return pltpu.HBM(shape, dtype) if i in hbm_outs else pltpu.VMEM(shape, dtype)

    kept = () if hbm_outs is None else hbm_outs

    def run(*args):
        args = [pltpu.with_memory_space_constraint(x, pltpu.HBM) if i in hbm else x for i, x in enumerate(args)]
        return pl.pallas_call(
            kernel,
            out_shape=[shape_of(i, shape, dtype) for i, (shape, dtype) in enumerate(outs)],
            in_specs=[pl.BlockSpec(memory_space=pltpu.HBM if i in hbm else pltpu.VMEM) for i in range(len(args))],
            out_specs=[pl.BlockSpec(memory_space=pltpu.HBM if i in kept else pltpu.VMEM) for i in range(len(outs))],
            scratch_shapes=list(scratch),
            compiler_params=pltpu.CompilerParams(vmem_limit_bytes=limit << 20),
            cost_estimate=pl.CostEstimate(flops=flops, bytes_accessed=moved, transcendentals=0),
        )(*args)

    return run


def blocks_of(slot):
    place = {}
    for axis in reversed(EXPERT):
        slot, place[axis] = divmod(slot, CUT[axis])
    found = []
    for place["y_hi"] in range(CUT["y_hi"]):
        block = 0
        for axis in CHIPS:
            block = block * CUT[axis] + (place[axis] - ROOT[axis]) % CUT[axis]
        found.append(block)
    return found


def to_blocks(scratch, values, first, rows, start=0):
    for k in range(values.shape[1] // LANES):
        scratch[pl.ds(start + first + k, rows, stride=16), :] = values[:, k * LANES : (k + 1) * LANES]


PIECES = 4


def front_kernel(tokens_in, grads_in, param_in, up_in, down_in, rows, dispatch, combine, tokens, grads, up, down, param, lines, sems):
    slots, width = param.shape
    count = tokens.shape[0]
    piece = count // PIECES
    copies = [pltpu.make_async_copy(param_in, param, sems.at[2 * PIECES])]
    for j, (source, target) in enumerate(((tokens_in, tokens), (grads_in, grads))):
        for p in range(PIECES):
            part = pl.ds(p * piece, piece)
            copies.append(pltpu.make_async_copy(source.at[part], target.at[part], sems.at[j * PIECES + p]))
    copies.append(pltpu.make_async_copy(up_in, up, sems.at[2 * PIECES + 1]))
    copies.append(pltpu.make_async_copy(down_in, down, sems.at[2 * PIECES + 2]))
    for copy in copies:
        copy.start()
    copies[0].wait()
    for p in range(PIECES):
        copies[1 + p].wait()
    logits = dot(param[...], tokens[...], ((1,), (1,)))
    e = jnp.exp(logits - jnp.max(logits, axis=1, keepdims=True))
    d = e / jnp.sum(e, axis=1, keepdims=True)
    e = jnp.exp(logits - jnp.max(logits, axis=0, keepdims=True))
    c = e / jnp.sum(e, axis=0, keepdims=True)
    dispatch[...] = d
    combine[...] = c
    to_blocks(lines, dot(d.astype(BF16), tokens[...], ((1,), (0,))), 0, slots)
    for p in range(PIECES):
        copies[1 + PIECES + p].wait()
    to_blocks(lines, dot(c.astype(BF16), grads[...], ((1,), (0,))), 8, slots)
    for slot in range(slots):
        for block in blocks_of(slot):
            rows[block] = lines[slot * 16 : slot * 16 + 16, :].astype(BF16)
    for copy in copies[1 + 2 * PIECES :]:
        copy.wait()


def expert_kernel(mine, up_own, up_other, down_own, down_other, back, keep, swap, parts, lines, sems):
    images = mine.shape[0]
    width, hidden = up_own.shape
    blocks = mine[...]
    parts[0] = blocks[:, :8].reshape(images, width)
    parts[1] = blocks[:, 8:].reshape(images, width)
    copies = [
        pltpu.make_async_copy(parts.at[pl.ds(0, 4)], swap, sems.at[0]),
        pltpu.make_async_copy(parts.at[pl.ds(4, 2)], keep, sems.at[1]),
    ]
    rows_in = parts[0]
    rows_grad = parts[1]
    for up, down, first in ((up_other, down_other, 2), (up_own, down_own, 4)):
        for c in range(0, hidden, 256):
            cols = slice(c, c + 256)
            v = dot(rows_in, up[:, cols], ((1,), (0,)))
            tangent = jnp.tanh(gelu_coeff * (v + cubic_coeff * v * v * v))
            parts[first, :, cols] = (0.5 * v * (1.0 + tangent)).astype(BF16)
            slope = 0.5 * (1.0 + tangent) + 0.5 * v * (1.0 - tangent * tangent) * gelu_coeff * (
                1.0 + 3.0 * cubic_coeff * v * v
            )
            g = dot(rows_grad, down[cols, :], ((1,), (1,)))
            parts[first + 1, :, cols] = (g * slope).astype(BF16)
        copies[first // 2 - 1].start()
    for n in range(0, width, 256):
        cols = slice(n, n + 256)
        out = dot(parts[4], down_own[:, cols], ((1,), (0,))) + dot(parts[2], down_other[:, cols], ((1,), (0,)))
        to_blocks(lines, out, n // LANES, images)
        out = dot(parts[5], up_own[cols, :], ((1,), (1,))) + dot(parts[3], up_other[cols, :], ((1,), (1,)))
        to_blocks(lines, out, 8 + n // LANES, images)
    back[...] = lines[: images * 16, :].reshape(images, 16, LANES).astype(BF16)
    for copy in copies:
        copy.wait()


def weights_kernel(keep, swap, recv, grad_up, grad_down):
    step = grad_up.shape[0]
    cols = pl.ds(pl.multiple_of(pl.program_id(0) * step, step), step)
    both = lambda a, b: jnp.concatenate([a, b], axis=0)
    rows_in = both(swap[0, :, cols], recv[0, :, cols])
    grad_up[...] = dot(rows_in, both(keep[1], recv[3]), ((0,), (0,))).astype(BF16)
    active = both(keep[0, :, cols], recv[2, :, cols])
    grad_down[...] = dot(active, both(swap[1], recv[1]), ((0,), (0,))).astype(BF16)


def weight_grads(keep, swap, recv):
    images, width = swap.shape[1:]
    step = 256
    whole = lambda n: pl.BlockSpec((n, images, width), lambda i: (0, 0, 0))
    return pl.pallas_call(
        weights_kernel,
        grid=(width // step,),
        out_shape=[jax.ShapeDtypeStruct((width, width), BF16)] * 2,
        in_specs=[whole(2), whole(4), whole(4)],
        out_specs=[pl.BlockSpec((step, width), lambda i: (i, 0))] * 2,
        compiler_params=pltpu.CompilerParams(vmem_limit_bytes=12 << 20),
        cost_estimate=pl.CostEstimate(
            flops=8 * images * width * width, bytes_accessed=4 * width * width, transcendentals=0
        ),
    )(keep, swap, recv)


def back_kernel(returned, tokens, grads, dispatch, combine, logit_grads, slot_grads, blocks, lines):
    slots = logit_grads.shape[0]
    width = tokens.shape[1]
    for slot in range(slots):
        lines[slot * 16 : slot * 16 + 16, :] = sum(returned[block].astype(F32) for block in blocks_of(slot))
    outputs = []
    for k in range(width // LANES):
        outputs.append(lines[pl.ds(k, slots, stride=16), :].astype(BF16))
        slot_grads[:, k * LANES : (k + 1) * LANES] = lines[pl.ds(8 + k, slots, stride=16), :].astype(BF16)
    c = combine[...]
    g = dot(jnp.concatenate(outputs, axis=1), grads[...], ((1,), (1,)))
    change = c * (g - jnp.sum(c * g, axis=0, keepdims=True))
    d = dispatch[...]
    g = dot(slot_grads[...], tokens[...], ((1,), (1,)))
    change = change + d * (g - jnp.sum(d * g, axis=1, keepdims=True))
    change = change.astype(BF16)
    logit_grads[...] = change
    term = dot(change, tokens[...], ((1,), (0,)))
    for first, row, col in tiles(slots, width):
        blocks[first : first + 16, :] = term[row : row + 16, col : col + LANES].astype(BF16)


def tiles(slots, width):
    first = 0
    for row in range(0, slots, 16):
        for col in range(0, width, LANES):
            yield first, row, col
            first += 16


def image_kernel(dispatch, logit_grads, slot_grads, param, grad_image):
    left = jnp.concatenate([dispatch[...].astype(BF16), logit_grads[...]], axis=0)
    right = jnp.concatenate([slot_grads[...], param[...]], axis=0)
    grad_image[...] = dot(left, right, ((0,), (0,))).astype(BF16)


def add_kernel(a, b, out):
    out[...] = a[...] + b[...]


def sum_kernel(blocks, out):
    total = jnp.sum(blocks[...].astype(F32), axis=0)
    out[...] = jnp.broadcast_to(total.astype(out.dtype)[None], out.shape)


def last_kernel(blocks, out):
    for first, row, col in tiles(*out.shape):
        out[row : row + 16, col : col + LANES] = blocks[first : first + 16, :].astype(F32)


def shards(tokens, slot_param, up_weight, down_weight, grad_output):
    image_tokens = tokens[0]
    image_grads = grad_output[0]
    up = up_weight[0]
    down = down_weight[0]
    count, width = image_tokens.shape
    hidden = up.shape[1]
    chips = lax.axis_size(CHIPS)
    slots = slot_param.shape[1]
    param = slot_param.T
    up_other = swap_cores(up)
    down_other = swap_cores(down)
    rows, dispatch, combine, image_tokens, image_grads, up_own, down_own = call(
        front_kernel,
        [((chips, 16, LANES), BF16), ((slots, count), F32), ((slots, count), F32)]
        + [((count, width), BF16)] * 2
        + [((width, hidden), BF16), ((hidden, width), BF16)],
        [
            pltpu.VMEM((slots, width), BF16),
            pltpu.VMEM((slots * 16 + 16, LANES), F32),
            pltpu.SemaphoreType.DMA((2 * PIECES + 3,)),
        ],
        flops=6 * slots * count * width,
        moved=16 * width * hidden,
        hbm=(0, 1, 2, 3, 4),
    )(image_tokens, image_grads, param, up, down)
    mine = exchange(rows, CHIPS)
    back, keep, swap = call(
        expert_kernel,
        [((chips, 16, LANES), BF16), ((2, chips, width), BF16), ((4, chips, width), BF16)],
        [
            pltpu.VMEM((6, chips, width), BF16),
            pltpu.VMEM((chips * 16 + 16, LANES), F32),
            pltpu.SemaphoreType.DMA((2,)),
        ],
        flops=16 * chips * width * hidden,
        moved=4 * width * hidden,
        hbm_outs=(1, 2),
        limit=8,
    )(mine, up_own, up_other, down_own, down_other)
    returned = exchange(back, CHIPS)
    lines = slots * width // LANES
    logit_grads, slot_grads, blocks = call(
        back_kernel,
        [((slots, count), BF16), ((slots, width), BF16), ((lines, LANES), BF16)],
        [pltpu.VMEM((slots * 16 + 16, LANES), F32)],
        flops=6 * slots * count * width,
        moved=6 * count * width,
    )(returned, image_tokens, image_grads, dispatch, combine)
    plane = lax.axis_size(PLANE)
    depth = lax.axis_size("z")
    blocks = exchange(blocks.reshape(plane, lines // plane, LANES), PLANE)
    (blocks,) = call(sum_kernel, [((depth, lines // plane, LANES), F32)])(blocks)
    blocks = exchange(blocks, ("z",))
    blocks, keep, swap, logit_grads, slot_grads = lax.optimization_barrier(
        (blocks, keep, swap, logit_grads, slot_grads)
    )
    recv = swap_cores(swap)
    (blocks,) = call(sum_kernel, [((plane, lines // plane, LANES), BF16)])(blocks)
    blocks = exchange(blocks, PLANE).reshape(lines, LANES)
    grad_up, grad_down = weight_grads(keep, swap, recv)
    (grad_image,) = call(
        image_kernel,
        [((count, width), BF16)],
        flops=4 * slots * count * width,
        moved=4 * count * width,
        hbm_outs=None,
    )(dispatch, logit_grads, slot_grads, param)
    blocks, grad_image, grad_up, grad_down = lax.optimization_barrier((blocks, grad_image, grad_up, grad_down))
    (param_grad,) = call(last_kernel, [((slots, width), F32)], hbm_outs=None)(blocks)
    return (grad_image[None], param_grad.T, grad_up[None], grad_down[None])


def solution(mesh):
    cut = Mesh(mesh.devices.reshape(tuple(CUT.values())), tuple(CUT))
    return jax.shard_map(
        shards,
        mesh=cut,
        in_specs=(
            P(EXPERT + DP, None, None),
            P(),
            P(EXPERT, None, DP),
            P(EXPERT, DP, None),
            P(EXPERT + DP, None, None),
        ),
        out_specs=(
            P(EXPERT + DP, None, None),
            P(),
            P(EXPERT, None, DP),
            P(EXPERT, DP, None),
        ),
        check_vma=False,
    )
```

```python
import math

import jax
import jax.numpy as jnp
import numpy as np
from jax import lax
from jax.experimental import pallas as pl
from jax.experimental.pallas import tpu as pltpu
from jax.sharding import Mesh, PartitionSpec as P

gelu_coeff = 0.7978845608
cubic_coeff = 0.044715

CUT = {"x": 4, "y_lo": 2, "z": 8, "y_hi": 2, "core": 2}
CHIPS = ("y_hi", "y_lo", "z", "x")
ROOT = {"x": 2, "y_lo": 0, "z": 6, "y_hi": 1}
EXPERT = ("x", "y_lo", "z")
DP = ("y_hi", "core")
PLANE = ("x", "y_lo", "y_hi", "core")
F32 = jnp.float32
BF16 = jnp.bfloat16
LANES = 128


def dot(a, b, dims):
    return lax.dot_general(a, b, (dims, ((), ())), preferred_element_type=F32)


def swap_cores(values):
    return lax.ppermute(values, "core", [(0, 1), (1, 0)])


def exchange(blocks, axes):
    numbers = np.arange(math.prod(CUT.values())).reshape(tuple(CUT.values()))
    for axis, first in ROOT.items():
        numbers = np.roll(numbers, -first, axis=list(CUT).index(axis))
    order = [axis for axis in CUT if axis not in axes] + list(axes)
    numbers = numbers.transpose([list(CUT).index(axis) for axis in order])
    groups = numbers.reshape(-1, math.prod(CUT[axis] for axis in axes)).tolist()
    return lax.all_to_all(blocks, tuple(CUT), 0, 0, axis_index_groups=groups, tiled=True)


def call(kernel, outs, scratch=(), flops=0, moved=0, hbm=(), hbm_outs=(), limit=4):
    def shape_of(i, shape, dtype):
        if hbm_outs is None:
            return jax.ShapeDtypeStruct(shape, dtype)
        return pltpu.HBM(shape, dtype) if i in hbm_outs else pltpu.VMEM(shape, dtype)

    kept = () if hbm_outs is None else hbm_outs

    def run(*args):
        args = [pltpu.with_memory_space_constraint(x, pltpu.HBM) if i in hbm else x for i, x in enumerate(args)]
        return pl.pallas_call(
            kernel,
            out_shape=[shape_of(i, shape, dtype) for i, (shape, dtype) in enumerate(outs)],
            in_specs=[pl.BlockSpec(memory_space=pltpu.HBM if i in hbm else pltpu.VMEM) for i in range(len(args))],
            out_specs=[pl.BlockSpec(memory_space=pltpu.HBM if i in kept else pltpu.VMEM) for i in range(len(outs))],
            scratch_shapes=list(scratch),
            compiler_params=pltpu.CompilerParams(vmem_limit_bytes=limit << 20),
            cost_estimate=pl.CostEstimate(flops=flops, bytes_accessed=moved, transcendentals=0),
        )(*args)

    return run


def blocks_of(slot):
    place = {}
    for axis in reversed(EXPERT):
        slot, place[axis] = divmod(slot, CUT[axis])
    found = []
    for place["y_hi"] in range(CUT["y_hi"]):
        block = 0
        for axis in CHIPS:
            block = block * CUT[axis] + (place[axis] - ROOT[axis]) % CUT[axis]
        found.append(block)
    return found


def to_blocks(scratch, values, first, rows, start=0):
    for k in range(values.shape[1] // LANES):
        scratch[pl.ds(start + first + k, rows, stride=16), :] = values[:, k * LANES : (k + 1) * LANES]


PIECES = 4


def front_kernel(tokens_in, grads_in, param_in, up_in, down_in, rows, dispatch, combine, tokens, grads, up, down, param, lines, sems):
    slots, width = param.shape
    count = tokens.shape[0]
    piece = count // PIECES
    copies = [pltpu.make_async_copy(param_in, param, sems.at[2 * PIECES])]
    for j, (source, target) in enumerate(((tokens_in, tokens), (grads_in, grads))):
        for p in range(PIECES):
            part = pl.ds(p * piece, piece)
            copies.append(pltpu.make_async_copy(source.at[part], target.at[part], sems.at[j * PIECES + p]))
    copies.append(pltpu.make_async_copy(up_in, up, sems.at[2 * PIECES + 1]))
    copies.append(pltpu.make_async_copy(down_in, down, sems.at[2 * PIECES + 2]))
    for copy in copies:
        copy.start()
    copies[0].wait()
    for p in range(PIECES):
        copies[1 + p].wait()
    logits = dot(param[...], tokens[...], ((1,), (1,)))
    e = jnp.exp(logits - jnp.max(logits, axis=1, keepdims=True))
    d = e / jnp.sum(e, axis=1, keepdims=True)
    e = jnp.exp(logits - jnp.max(logits, axis=0, keepdims=True))
    c = e / jnp.sum(e, axis=0, keepdims=True)
    dispatch[...] = d
    combine[...] = c
    to_blocks(lines, dot(d.astype(BF16), tokens[...], ((1,), (0,))), 0, slots)
    for p in range(PIECES):
        copies[1 + PIECES + p].wait()
    to_blocks(lines, dot(c.astype(BF16), grads[...], ((1,), (0,))), 8, slots)
    for slot in range(slots):
        for block in blocks_of(slot):
            rows[block] = lines[slot * 16 : slot * 16 + 16, :].astype(BF16)
    for copy in copies[1 + 2 * PIECES :]:
        copy.wait()


def expert_kernel(mine, up_own, up_other, down_own, down_other, back, keep, swap, parts, lines, sems):
    images = mine.shape[0]
    width, hidden = up_own.shape
    blocks = mine[...]
    parts[0] = blocks[:, :8].reshape(images, width)
    parts[1] = blocks[:, 8:].reshape(images, width)
    copies = [
        pltpu.make_async_copy(parts.at[pl.ds(0, 4)], swap, sems.at[0]),
        pltpu.make_async_copy(parts.at[pl.ds(4, 2)], keep, sems.at[1]),
    ]
    rows_in = parts[0]
    rows_grad = parts[1]
    for up, down, first in ((up_other, down_other, 2), (up_own, down_own, 4)):
        for c in range(0, hidden, 256):
            cols = slice(c, c + 256)
            v = dot(rows_in, up[:, cols], ((1,), (0,)))
            tangent = jnp.tanh(gelu_coeff * (v + cubic_coeff * v * v * v))
            parts[first, :, cols] = (0.5 * v * (1.0 + tangent)).astype(BF16)
            slope = 0.5 * (1.0 + tangent) + 0.5 * v * (1.0 - tangent * tangent) * gelu_coeff * (
                1.0 + 3.0 * cubic_coeff * v * v
            )
            g = dot(rows_grad, down[cols, :], ((1,), (1,)))
            parts[first + 1, :, cols] = (g * slope).astype(BF16)
        copies[first // 2 - 1].start()
    for n in range(0, width, 256):
        cols = slice(n, n + 256)
        out = dot(parts[4], down_own[:, cols], ((1,), (0,))) + dot(parts[2], down_other[:, cols], ((1,), (0,)))
        to_blocks(lines, out, n // LANES, images)
        out = dot(parts[5], up_own[cols, :], ((1,), (1,))) + dot(parts[3], up_other[cols, :], ((1,), (1,)))
        to_blocks(lines, out, 8 + n // LANES, images)
    back[...] = lines[: images * 16, :].reshape(images, 16, LANES).astype(BF16)
    for copy in copies:
        copy.wait()


def weights_kernel(keep, swap, recv, grad_up, grad_down):
    step = grad_up.shape[0]
    cols = pl.ds(pl.multiple_of(pl.program_id(0) * step, step), step)
    both = lambda a, b: jnp.concatenate([a, b], axis=0)
    rows_in = both(swap[0, :, cols], recv[0, :, cols])
    grad_up[...] = dot(rows_in, both(keep[1], recv[3]), ((0,), (0,))).astype(BF16)
    active = both(keep[0, :, cols], recv[2, :, cols])
    grad_down[...] = dot(active, both(swap[1], recv[1]), ((0,), (0,))).astype(BF16)


def weight_grads(keep, swap, recv):
    images, width = swap.shape[1:]
    step = 256
    whole = lambda n: pl.BlockSpec((n, images, width), lambda i: (0, 0, 0))
    return pl.pallas_call(
        weights_kernel,
        grid=(width // step,),
        out_shape=[jax.ShapeDtypeStruct((width, width), BF16)] * 2,
        in_specs=[whole(2), whole(4), whole(4)],
        out_specs=[pl.BlockSpec((step, width), lambda i: (i, 0))] * 2,
        compiler_params=pltpu.CompilerParams(vmem_limit_bytes=12 << 20),
        cost_estimate=pl.CostEstimate(
            flops=8 * images * width * width, bytes_accessed=4 * width * width, transcendentals=0
        ),
    )(keep, swap, recv)


def back_kernel(returned, tokens, grads, dispatch, combine, logit_grads, slot_grads, blocks, lines):
    slots = logit_grads.shape[0]
    width = tokens.shape[1]
    for slot in range(slots):
        lines[slot * 16 : slot * 16 + 16, :] = sum(returned[block].astype(F32) for block in blocks_of(slot))
    outputs = []
    for k in range(width // LANES):
        outputs.append(lines[pl.ds(k, slots, stride=16), :].astype(BF16))
        slot_grads[:, k * LANES : (k + 1) * LANES] = lines[pl.ds(8 + k, slots, stride=16), :].astype(BF16)
    c = combine[...]
    g = dot(jnp.concatenate(outputs, axis=1), grads[...], ((1,), (1,)))
    change = c * (g - jnp.sum(c * g, axis=0, keepdims=True))
    d = dispatch[...]
    g = dot(slot_grads[...], tokens[...], ((1,), (1,)))
    change = change + d * (g - jnp.sum(d * g, axis=1, keepdims=True))
    change = change.astype(BF16)
    logit_grads[...] = change
    term = dot(change, tokens[...], ((1,), (0,)))
    for first, row, col in tiles(slots, width):
        blocks[first : first + 16, :] = term[row : row + 16, col : col + LANES].astype(BF16)


def tiles(slots, width):
    first = 0
    for row in range(0, slots, 16):
        for col in range(0, width, LANES):
            yield first, row, col
            first += 16


def image_kernel(dispatch, logit_grads, slot_grads, param, grad_image):
    left = jnp.concatenate([dispatch[...].astype(BF16), logit_grads[...]], axis=0)
    right = jnp.concatenate([slot_grads[...], param[...]], axis=0)
    grad_image[...] = dot(left, right, ((0,), (0,))).astype(BF16)


def add_kernel(a, b, out):
    out[...] = a[...] + b[...]


def sum_kernel(blocks, out):
    total = jnp.sum(blocks[...].astype(F32), axis=0)
    out[...] = jnp.broadcast_to(total.astype(out.dtype)[None], out.shape)


def last_kernel(blocks, out):
    for first, row, col in tiles(*out.shape):
        out[row : row + 16, col : col + LANES] = blocks[first : first + 16, :].astype(F32)


def shards(tokens, slot_param, up_weight, down_weight, grad_output):
    image_tokens = tokens[0]
    image_grads = grad_output[0]
    up = up_weight[0]
    down = down_weight[0]
    count, width = image_tokens.shape
    hidden = up.shape[1]
    chips = lax.axis_size(CHIPS)
    slots = slot_param.shape[1]
    param = slot_param.T
    up_other = swap_cores(up)
    down_other = swap_cores(down)
    rows, dispatch, combine, image_tokens, image_grads, up_own, down_own = call(
        front_kernel,
        [((chips, 16, LANES), BF16), ((slots, count), F32), ((slots, count), F32)]
        + [((count, width), BF16)] * 2
        + [((width, hidden), BF16), ((hidden, width), BF16)],
        [
            pltpu.VMEM((slots, width), BF16),
            pltpu.VMEM((slots * 16 + 16, LANES), F32),
            pltpu.SemaphoreType.DMA((2 * PIECES + 3,)),
        ],
        flops=6 * slots * count * width,
        moved=16 * width * hidden,
        hbm=(0, 1, 2, 3, 4),
    )(image_tokens, image_grads, param, up, down)
    mine = exchange(rows, CHIPS)
    back, keep, swap = call(
        expert_kernel,
        [((chips, 16, LANES), BF16), ((2, chips, width), BF16), ((4, chips, width), BF16)],
        [
            pltpu.VMEM((6, chips, width), BF16),
            pltpu.VMEM((chips * 16 + 16, LANES), F32),
            pltpu.SemaphoreType.DMA((2,)),
        ],
        flops=16 * chips * width * hidden,
        moved=4 * width * hidden,
        hbm_outs=(1, 2),
        limit=8,
    )(mine, up_own, up_other, down_own, down_other)
    returned = exchange(back, CHIPS)
    lines = slots * width // LANES
    logit_grads, slot_grads, blocks = call(
        back_kernel,
        [((slots, count), BF16), ((slots, width), BF16), ((lines, LANES), BF16)],
        [pltpu.VMEM((slots * 16 + 16, LANES), F32)],
        flops=6 * slots * count * width,
        moved=6 * count * width,
    )(returned, image_tokens, image_grads, dispatch, combine)
    plane = lax.axis_size(PLANE)
    depth = lax.axis_size("z")
    blocks = exchange(blocks.reshape(plane, lines // plane, LANES), PLANE)
    blocks, logit_grads, slot_grads = lax.optimization_barrier((blocks, logit_grads, slot_grads))
    (blocks,) = call(sum_kernel, [((depth, lines // plane, LANES), F32)])(blocks)
    (grad_image,) = call(
        image_kernel,
        [((count, width), BF16)],
        flops=4 * slots * count * width,
        moved=4 * count * width,
        hbm_outs=None,
    )(dispatch, logit_grads, slot_grads, param)
    blocks = exchange(blocks, ("z",))
    blocks, grad_image, keep, swap = lax.optimization_barrier((blocks, grad_image, keep, swap))
    recv = swap_cores(swap)
    (blocks,) = call(sum_kernel, [((plane, lines // plane, LANES), BF16)])(blocks)
    blocks = exchange(blocks, PLANE).reshape(lines, LANES)
    grad_up, grad_down = weight_grads(keep, swap, recv)
    blocks, grad_up, grad_down = lax.optimization_barrier((blocks, grad_up, grad_down))
    (param_grad,) = call(last_kernel, [((slots, width), F32)], hbm_outs=None)(blocks)
    return (grad_image[None], param_grad.T, grad_up[None], grad_down[None])


def solution(mesh):
    cut = Mesh(mesh.devices.reshape(tuple(CUT.values())), tuple(CUT))
    return jax.shard_map(
        shards,
        mesh=cut,
        in_specs=(
            P(EXPERT + DP, None, None),
            P(),
            P(EXPERT, None, DP),
            P(EXPERT, DP, None),
            P(EXPERT + DP, None, None),
        ),
        out_specs=(
            P(EXPERT + DP, None, None),
            P(),
            P(EXPERT, None, DP),
            P(EXPERT, DP, None),
        ),
        check_vma=False,
    )
```
